256 devices in a mesh: head: 8 (over x, y_lo), inner: 8 (over z), outer: 4 (over y_hi, core).
Axes of the slice: x: 4, y: 4 (y_hi: 2, y_lo: 2; y = y_hi * 2 + y_lo), z: 8, core: 2. Of those that a mesh axis runs over, the one named last changes fastest.
Arguments:
- queries: bfloat16 [4096, 8192], P(('inner', 'outer'), 'head'), may hold values from -100 to 100
- keys: bfloat16 [4096, 1024], P(('inner', 'outer'), 'head'), may hold values from -4 to 4
- values: bfloat16 [4096, 1024], P(('inner', 'outer'), 'head'), may hold values from -6 to 6
- output_gradient: bfloat16 [4096, 8192], P(('inner', 'outer'), 'head'), may hold values from -6 to 6
- block_perm: int32 [64], replicated, may hold values from 0 to 63, as said below
- segment_ids: int32 [4096], replicated, may hold values from 0 to 3, as said below
Outputs:
- attended: bfloat16 [4096, 8192], P(('inner', 'outer'), 'head')
- query_grad: bfloat16 [4096, 8192], P(('inner', 'outer'), 'head')
- key_grad: bfloat16 [4096, 1024], P(('inner', 'outer'), 'head')
- value_grad: bfloat16 [4096, 1024], P(('inner', 'outer'), 'head')
The draws below stay inside these ranges and needn't reach their ends.
Inputs may be any that keep to these rules, and one draw needn't show every extreme that they name: `block_perm`: each of 0 to 63 exactly once. `segment_ids`: document ids never fall along the rollout order.
All inputs are finite; a program needn't handle non-finite values.
Results may differ from the reference program's by a relative error of at most 0.039.
Values may be sent and summed in bfloat16 or wider, within the bound.
No kernel may reach another device: no remote copies, remote signals or barrier semaphores. Data moves between devices by JAX's collectives and lax.ppermute only.
A program may use at most 64 MiB of HBM per device.

```python
import math
import jax
import jax.numpy as jnp
from jax import lax

QUERY_HEADS = 64
KEY_VALUE_HEADS = 8
HEAD_DIMENSION = 128
DOCS = 4
SEQUENCE_TOKENS = 4096
BLOCK = 64
NBLK = 64


def block_order(key):
    return jax.random.permutation(jax.random.fold_in(key, 101), NBLK).astype(jnp.int32)


def raw_keys(key):
    return jnp.clip(jax.random.normal(jax.random.fold_in(key, 202), (SEQUENCE_TOKENS, KEY_VALUE_HEADS, HEAD_DIMENSION), jnp.float32), -4.0, 4.0)


def into_saved_layout(table, visit_sequence):
    return table.reshape(NBLK, BLOCK, -1)[visit_sequence].reshape(SEQUENCE_TOKENS, -1)


def draw_block_perm(key, part):
    return block_order(key)


def draw_segment_ids(key, part):
    key = jax.random.fold_in(key, 3)
    cuts = jax.random.randint(key, (DOCS - 1,), SEQUENCE_TOKENS // 8, SEQUENCE_TOKENS)
    spots = jnp.arange(SEQUENCE_TOKENS, dtype=jnp.int32)
    return jnp.sum((spots[:, None] >= cuts[None, :]).astype(jnp.int32), axis=1).astype(jnp.int32)


def draw_keys(key, part):
    visit_sequence = block_order(key)
    start_offset = raw_keys(key)
    return into_saved_layout(start_offset.reshape(SEQUENCE_TOKENS, KEY_VALUE_HEADS * HEAD_DIMENSION), visit_sequence).astype(jnp.bfloat16)


def draw_queries(key, part):
    visit_sequence = block_order(key)
    key = jax.random.fold_in(key, 5)
    fresh = jnp.clip(jax.random.normal(key, (SEQUENCE_TOKENS, QUERY_HEADS, HEAD_DIMENSION), jnp.float32), -4.0, 4.0)
    return into_saved_layout(fresh.reshape(SEQUENCE_TOKENS, QUERY_HEADS * HEAD_DIMENSION), visit_sequence).astype(jnp.bfloat16)


def level_of(key, extent, cuts, least, top_value):
    level, own = 1.0, jax.random.fold_in(key, 6)
    for position, blocks in cuts:
        steps = jnp.exp(jax.random.uniform(jax.random.fold_in(own, position), (blocks,), jnp.float32, least / len(cuts), top_value / len(cuts)))
        level = level * jnp.repeat(steps, extent[position] // blocks).reshape([-1 if axis == position else 1 for axis in range(len(extent))])
    return level


def noise(stream_key, dims, spread, reach, shards=(), held_as=jnp.bfloat16):
    array = spread * jax.random.normal(stream_key, dims, jnp.float32)
    if shards:
        array = array * level_of(stream_key, dims, shards, -0.22, 0.18)
    return jnp.clip(array, -reach, reach).astype(held_as)


def setup_inputs(seed: int = 0) -> dict:
    seeds = jax.random.split(jax.random.key(seed), 7)
    return {
        "queries": draw_queries(jax.random.fold_in(seeds[6], 71), 0),
        "keys": draw_keys(jax.random.fold_in(seeds[6], 71), 0),
        "values": noise(seeds[2], (SEQUENCE_TOKENS, KEY_VALUE_HEADS * HEAD_DIMENSION), 1.0, 6.0, ((0, 32), (1, 8))),
        "output_gradient": noise(seeds[3], (SEQUENCE_TOKENS, QUERY_HEADS * HEAD_DIMENSION), 1.0, 6.0, ((0, 32), (1, 8))),
        "block_perm": draw_block_perm(jax.random.fold_in(seeds[6], 71), 0),
        "segment_ids": draw_segment_ids(jax.random.fold_in(seeds[6], 71), 0),
    }


def reference(queries, keys, values, output_gradient, block_perm, segment_ids):
    scale = 1.0 / math.sqrt(HEAD_DIMENSION)
    group_index = QUERY_HEADS // KEY_VALUE_HEADS
    qblock = min(SEQUENCE_TOKENS, 512)
    nq = SEQUENCE_TOKENS // qblock
    positions = (block_perm[:, None] * BLOCK + jnp.arange(BLOCK, dtype=jnp.int32)[None, :]).reshape(SEQUENCE_TOKENS).astype(jnp.int32)
    documents = segment_ids.reshape(NBLK, BLOCK)[block_perm].reshape(SEQUENCE_TOKENS).astype(jnp.int32)
    query_head_rows = jnp.moveaxis(queries.reshape(SEQUENCE_TOKENS, group_index, KEY_VALUE_HEADS, HEAD_DIMENSION), 2, 0)
    gradient_heads = jnp.moveaxis(output_gradient.reshape(SEQUENCE_TOKENS, group_index, KEY_VALUE_HEADS, HEAD_DIMENSION), 2, 0)
    key_head_rows = jnp.moveaxis(keys.reshape(SEQUENCE_TOKENS, KEY_VALUE_HEADS, HEAD_DIMENSION), 1, 0)
    value_head_rows = jnp.moveaxis(values.reshape(SEQUENCE_TOKENS, KEY_VALUE_HEADS, HEAD_DIMENSION), 1, 0)

    def per_head(inputs):
        qh, gh, kh, vh = inputs
        kf = kh.astype(jnp.float32)
        vf = vh.astype(jnp.float32)

        def step(carry, blockin):
            dk_acc, dv_acc = carry
            qb, gb, posb, docb = blockin
            qf = qb.astype(jnp.float32)
            gf = gb.astype(jnp.float32)
            logits = jnp.einsum('qgd,kd->qgk', qf, kf) * scale
            allowed = ((positions[None, :] <= posb[:, None]) & (documents[None, :] == docb[:, None]))[:, None, :]
            top = lax.optimization_barrier(jnp.max(jnp.where(allowed, logits, -1e+30), axis=-1))
            total = lax.optimization_barrier(jnp.sum(jnp.where(allowed, jnp.exp(logits - top[..., None]), 0.0), axis=-1))
            lse = top + jnp.log(total)
            probs = jnp.where(allowed, jnp.exp(logits - lse[..., None]), 0.0)
            probs_b = lax.optimization_barrier(probs.astype(jnp.bfloat16)).astype(jnp.float32)
            attended = jnp.einsum('qgk,kd->qgd', probs_b, vf).astype(jnp.bfloat16)
            att_f = lax.optimization_barrier(attended).astype(jnp.float32)
            delta = lax.optimization_barrier(jnp.sum(gf * att_f, axis=-1))
            dprobs = jnp.einsum('qgd,kd->qgk', gf, vf)
            dscore = probs * (dprobs - delta[..., None])
            dscore_b = lax.optimization_barrier(dscore.astype(jnp.bfloat16)).astype(jnp.float32)
            qgrad = (jnp.einsum('qgk,kd->qgd', dscore_b, kf) * scale).astype(jnp.bfloat16)
            dk_acc = dk_acc + jnp.einsum('qgk,qgd->kd', dscore_b, qf) * scale
            dv_acc = dv_acc + jnp.einsum('qgk,qgd->kd', probs_b, gf)
            return ((dk_acc, dv_acc), (attended, qgrad))
        blocks_in = (qh.reshape(nq, qblock, group_index, HEAD_DIMENSION), gh.reshape(nq, qblock, group_index, HEAD_DIMENSION), positions.reshape(nq, qblock), documents.reshape(nq, qblock))
        zeros = jnp.zeros((SEQUENCE_TOKENS, HEAD_DIMENSION), jnp.float32)
        (dk_acc, dv_acc), (attended, qgrad) = lax.scan(step, (zeros, zeros), blocks_in)
        return (attended.reshape(SEQUENCE_TOKENS, group_index, HEAD_DIMENSION), qgrad.reshape(SEQUENCE_TOKENS, group_index, HEAD_DIMENSION), dk_acc.astype(jnp.bfloat16), dv_acc.astype(jnp.bfloat16))
    attended, qgrad, key_gradient, value_gradient = lax.map(per_head, (query_head_rows, gradient_heads, key_head_rows, value_head_rows))
    attended = jnp.moveaxis(attended, 0, 2).reshape(SEQUENCE_TOKENS, QUERY_HEADS * HEAD_DIMENSION)
    qgrad = jnp.moveaxis(qgrad, 0, 2).reshape(SEQUENCE_TOKENS, QUERY_HEADS * HEAD_DIMENSION)
    key_gradient = jnp.moveaxis(key_gradient, 0, 1).reshape(SEQUENCE_TOKENS, KEY_VALUE_HEADS * HEAD_DIMENSION)
    value_gradient = jnp.moveaxis(value_gradient, 0, 1).reshape(SEQUENCE_TOKENS, KEY_VALUE_HEADS * HEAD_DIMENSION)
    return (attended, qgrad, key_gradient, value_gradient)
```

```python
import functools
import math

import jax
import jax.numpy as jnp
from jax import lax
from jax.experimental import pallas as pl
from jax.experimental.pallas import tpu as pltpu
from jax.sharding import PartitionSpec as P

HEAD = 128
GROUP = 8
BLOCK = 64
TILE = 4 * BLOCK
LANES = GROUP * BLOCK
CALL = 16
SCALE = 1.0 / math.sqrt(HEAD)
SCALE2 = SCALE * math.log2(math.e)
LOW = -1e30
NT = (((1,), (1,)), ((), ()))
TN = (((0,), (0,)), ((), ()))
NN = (((1,), (0,)), ((), ()))
F32, BF16 = jnp.float32, jnp.bfloat16


def mm(a, b, dims):
    return lax.dot_general(a, b, dims, preferred_element_type=F32)


def blocks_of(kinds, refs, meta):
    z, outer = meta[0], meta[1]
    core = lax.rem(outer, 2)
    for (side, steps), ref in zip(kinds, refs, strict=True):
        sign = (1 - 2 * core) * (1 if side == "near" else -1)
        chunk = lax.rem(z - sign * steps + 8, 8)
        base = outer if side == "near" else outer + 1 - 2 * core
        twin = base + 1 - 2 * lax.rem(base, 2)
        shards = [base, lax.rem(base + 2, 4), twin, lax.rem(twin + 2, 4)]
        for i in range(ref.shape[0]):
            for b in range(2):
                yield ref, i, b * BLOCK, chunk * 8 + shards[i] * 2 + b


def limits(perm, meta, qb):
    lane = lax.rem(lax.broadcasted_iota(jnp.int32, (1, LANES), 1), BLOCK)
    block = perm[meta[0] * 8 + meta[1] * 2 + qb]
    first = block * BLOCK
    qpos = first + lane
    low = jnp.zeros_like(qpos)
    low_first = jnp.int32(0)
    for d in range(3):
        start = meta[2 + d]
        low = jnp.where(start <= qpos, jnp.maximum(low, start), low)
        low_first = jnp.where(start <= first, jnp.maximum(low_first, start), low_first)
    return qpos, low, low_first // BLOCK, block


def pick(perm, found, lowest, highest, k_s, v_s, pos_s, slot_s):
    n = jnp.int32(0)
    for i, (ref, shard, row, stored) in enumerate(found):
        at = pl.ds(pl.multiple_of(n * BLOCK, BLOCK), BLOCK)
        k_s[at, :] = ref[shard, 0, row : row + BLOCK, :]
        v_s[at, :] = ref[shard, 1, row : row + BLOCK, :]
        position = perm[stored]
        pos_s[n] = position
        slot_s[n] = i
        n = n + jnp.where((position >= lowest) & (position <= highest), 1, 0)
    for j in range(3):
        at = pl.ds(pl.multiple_of((n + j) * BLOCK, BLOCK), BLOCK)
        k_s[at, :] = jnp.zeros((BLOCK, HEAD), BF16)
        v_s[at, :] = jnp.zeros((BLOCK, HEAD), BF16)
        pos_s[n + j] = 1 << 14
        slot_s[n + j] = CALL
    return (n + 3) // 4


def tile(t):
    return pl.ds(pl.multiple_of(t * TILE, TILE), TILE)


def masked_scores(t, q, qpos, low, k_s, pos_s):
    row = lax.broadcasted_iota(jnp.int32, (BLOCK, 1), 0)
    kpos = jnp.concatenate([pos_s[4 * t + j] * BLOCK + row for j in range(4)], axis=0)
    return jnp.where((kpos <= qpos) & (kpos >= low), mm(k_s[tile(t), :], q, NT), LOW)


def heads_of(qd, which, qb):
    return jnp.concatenate([qd[i, which, qb * BLOCK : (qb + 1) * BLOCK, :] for i in range(GROUP)], axis=0)


def eights(x):
    return x.reshape(TILE // 8, 8, LANES)


def forward_kernel(kinds, first, last, *refs):
    perm, meta, qd, *refs = refs
    pieces, refs = refs[: len(kinds)], refs[len(kinds) :]
    if not first:
        stat_in, ot_in, *refs = refs
    stat, ot, k_s, v_s, s_s, pos_s, slot_s, *work = refs
    found = list(blocks_of(kinds, pieces, meta))
    for qb in range(2):
        q = heads_of(qd, 0, qb)
        qpos, low, lowest, highest = limits(perm, meta, qb)
        tiles = pick(perm, found, lowest, highest, k_s, v_s, pos_s, slot_s)

        def scores(t, top):
            s = masked_scores(t, q, qpos, low, k_s, pos_s)
            s_s[tile(t), :] = s
            return jnp.maximum(top, jnp.max(eights(s), axis=0))

        before = jnp.full((8, LANES), LOW, F32) if first else stat_in[qb, 0]
        top = lax.fori_loop(0, tiles, scores, before)
        top = jnp.max(top, axis=0, keepdims=True)
        acc = work[0] if last else ot.at[qb]
        if first:
            acc[...] = jnp.zeros((HEAD, LANES), F32)
            total = jnp.zeros((8, LANES), F32)
        else:
            keep = jnp.exp2((before[:1] - top) * SCALE2)
            acc[...] = ot_in[qb] * keep
            total = stat_in[qb, 1] * keep

        def sums(t, total):
            p = jnp.exp2((s_s[tile(t), :] - top) * SCALE2)
            acc[...] += mm(v_s[tile(t), :], p.astype(BF16), TN)
            return total + jnp.sum(eights(p), axis=0)

        total = lax.fori_loop(0, tiles, sums, total)
        if not last:
            stat[qb, 0] = jnp.broadcast_to(top, (8, LANES))
            stat[qb, 1] = total
            continue
        total = jnp.sum(total, axis=0, keepdims=True)
        out_t = acc[...] * (1.0 / total)
        out = out_t.T.astype(BF16)
        for i in range(GROUP):
            ot[i, qb * BLOCK : (qb + 1) * BLOCK, :] = out[i * BLOCK : (i + 1) * BLOCK, :]
        grad_t = heads_of(qd, 1, qb).astype(F32).T
        delta = jnp.sum(grad_t * out_t.astype(BF16).astype(F32), axis=0, keepdims=True)
        stat[qb, 0] = jnp.broadcast_to(top * SCALE2 + jnp.log2(total), (8, LANES))
        stat[qb, 1] = jnp.broadcast_to(delta, (8, LANES))


def backward_kernel(kinds, first, last, *refs):
    perm, meta, qd, stat, *refs = refs
    pieces, refs = refs[: len(kinds)], refs[len(kinds) :]
    if not first:
        dqt_in, *refs = refs
    if last:
        out, *refs = refs
    grads, refs = refs[: len(kinds)], refs[len(kinds) :]
    dq, k_s, v_s, dk_s, dv_s, pos_s, slot_s, *work = refs
    found = list(blocks_of(kinds, pieces, meta))
    dk_s[...] = jnp.zeros_like(dk_s)
    dv_s[...] = jnp.zeros_like(dv_s)
    for qb in range(2):
        q, do = heads_of(qd, 0, qb), heads_of(qd, 1, qb)
        qpos, low, lowest, highest = limits(perm, meta, qb)
        tiles = pick(perm, found, lowest, highest, k_s, v_s, pos_s, slot_s)
        lse, delta = stat[qb, 0, :1, :], stat[qb, 1, :1, :]
        acc = work[0] if last else dq.at[qb]
        acc[...] = jnp.zeros((HEAD, LANES), F32) if first else dqt_in[qb]

        def step(t, carry):
            p = jnp.exp2(masked_scores(t, q, qpos, low, k_s, pos_s) * SCALE2 - lse)
            dp = mm(v_s[tile(t), :], do, NT)
            ds = (p * (dp - delta)).astype(BF16)
            dv = mm(p.astype(BF16), do, NN)
            dk = mm(ds, q, NN)
            acc[...] += mm(k_s[tile(t), :], ds, TN)
            for j in range(4):
                at = pl.ds(pl.multiple_of(slot_s[4 * t + j] * BLOCK, BLOCK), BLOCK)
                dk_s[at, :] += dk[j * BLOCK : (j + 1) * BLOCK, :]
                dv_s[at, :] += dv[j * BLOCK : (j + 1) * BLOCK, :]
            return carry

        lax.fori_loop(0, tiles, step, 0)
        if last:
            done = (acc[...] * SCALE).T.astype(BF16)
            for i in range(GROUP):
                rows = slice(qb * BLOCK, (qb + 1) * BLOCK)
                dq[i, 0, rows, :] = out[i, rows, :]
                dq[i, 1, rows, :] = done[i * BLOCK : (i + 1) * BLOCK, :]
    n = 0
    for grad in grads:
        for i in range(grad.shape[0]):
            for b in range(2):
                at, rows = slice(n * BLOCK, (n + 1) * BLOCK), slice(b * BLOCK, (b + 1) * BLOCK)
                grad[i, 0, rows, :] = (dk_s[at, :] * SCALE).astype(BF16)
                grad[i, 1, rows, :] = dv_s[at, :].astype(BF16)
                n += 1


VMEM = pl.BlockSpec(memory_space=pltpu.VMEM)
SMEM = pl.BlockSpec(memory_space=pltpu.SMEM)
STAT = jax.ShapeDtypeStruct((2, 2, 8, LANES), F32)
WIDE = jax.ShapeDtypeStruct((2, HEAD, LANES), F32)
PICKED = [pltpu.VMEM(((CALL + 4) * BLOCK, HEAD), BF16)] * 2
LISTS = [pltpu.SMEM((CALL + 4,), jnp.int32)] * 2


def call(kernel, operands, outs, scratch, flops):
    return pl.pallas_call(
        kernel,
        out_shape=outs,
        in_specs=[SMEM, SMEM] + [VMEM] * (len(operands) - 2),
        out_specs=[VMEM] * len(outs),
        scratch_shapes=scratch,
        compiler_params=pltpu.CompilerParams(vmem_limit_bytes=20 * 1024 * 1024),
        cost_estimate=pl.CostEstimate(flops=flops, bytes_accessed=2 * 10**6, transcendentals=10**6),
    )(*operands)


def forward(perm, meta, qd, kinds, pieces, state, last):
    first = state is None
    outs = [STAT, jax.ShapeDtypeStruct((GROUP, 128, HEAD), BF16) if last else WIDE]
    scratch = PICKED + [pltpu.VMEM(((CALL + 4) * BLOCK, LANES), F32)] + LISTS
    scratch += [pltpu.VMEM((HEAD, LANES), F32)] if last else []
    kernel = functools.partial(forward_kernel, kinds, first, last)
    return call(kernel, [perm, meta, qd, *pieces, *(state or [])], outs, scratch, 5 * 10**8)


def backward(perm, meta, qd, stat, kinds, pieces, dqt, out):
    first, last = dqt is None, out is not None
    outs = [jax.ShapeDtypeStruct(p.shape, BF16) for p in pieces]
    outs.append(jax.ShapeDtypeStruct((GROUP, 2, 128, HEAD), BF16) if last else WIDE)
    scratch = PICKED + [pltpu.VMEM(((CALL + 1) * BLOCK, HEAD), F32)] * 2 + LISTS
    scratch += [pltpu.VMEM((HEAD, LANES), F32)] if last else []
    operands = [perm, meta, qd, stat, *pieces] + ([] if first else [dqt]) + ([out] if last else [])
    return call(functools.partial(backward_kernel, kinds, first, last), operands, outs, scratch, 10**9)


def outer_perm(move):
    pairs = []
    for z in range(8):
        for y in range(2):
            for c in range(2):
                z2, y2, c2 = move(z, y, c)
                pairs.append((z * 4 + y * 2 + c, (z2 % 8) * 4 + y2 * 2 + c2))
    return pairs


AXES = ("inner", "outer")
CORE = outer_perm(lambda z, y, c: (z, y, 1 - c))
TWIN = outer_perm(lambda z, y, c: (z, 1 - y, c))
CROSS = outer_perm(lambda z, y, c: (z, 1 - y, 1 - c))
ONWARD = outer_perm(lambda z, y, c: (z + 1 - 2 * c, y, c))
HOMEWARD = outer_perm(lambda z, y, c: (z - 1 + 2 * c, y, c))


def send(x, pairs):
    return lax.ppermute(x, AXES, pairs)


def after(*values):
    return lax.optimization_barrier(values)


def total32(*terms):
    return sum(t.astype(F32) for t in terms)


def add(*terms):
    return total32(*terms).astype(BF16)


def on_device(queries, keys, values, output_gradient, block_perm, segment_ids):
    rows = queries.shape[0]
    kv = jnp.stack([keys, values])
    own = jnp.stack([kv, *(send(kv, pairs) for pairs in (TWIN, CORE, CROSS))])
    qd = jnp.stack([queries.reshape(rows, GROUP, HEAD), output_gradient.reshape(rows, GROUP, HEAD)])
    qd = lax.all_to_all(jnp.transpose(qd, (2, 0, 1, 3)), "head", 0, 0, tiled=True)
    starts = jnp.sum(segment_ids[None, :] < jnp.arange(1, 4, dtype=jnp.int32)[:, None], axis=1)
    place = jnp.stack([lax.axis_index("inner"), lax.axis_index("outer")])
    meta = jnp.concatenate([place.astype(jnp.int32), starts.astype(jnp.int32)])

    run = functools.partial(forward, block_perm, meta, qd)
    near1 = send(own, ONWARD)
    calls = [((("near", 0), ("near", 1)), (own, near1))]
    near2 = send(near1, ONWARD)
    far1 = send(near1, CORE)
    state = run(*calls[0], None, False)
    calls.append(((("far", 1), ("near", 2)), (far1, near2)))
    near3 = send(near2, ONWARD)
    far2 = send(near2, CORE)
    near3, *state = after(near3, *state)
    state = run(*calls[1], state, False)
    calls.append(((("far", 2), ("near", 3)), (far2, near3)))
    near4 = send(near3[:2], ONWARD)
    far3 = send(near3, CORE)
    state = run(*calls[2], state, False)
    near4, *state = after(near4, *state)
    far4 = send(near4, CORE)
    calls.append(((("far", 3), ("near", 4), ("far", 4)), (far3, near4, far4)))
    stat, out = run(*calls[3], state, True)

    run = functools.partial(backward, block_perm, meta, qd, stat)
    far3, near4, far4, dqt = run(*calls[3], None, None)
    far2, near3, dqt = run(*calls[2], dqt, None)
    moving = send(add(near4, send(far4, CORE)), HOMEWARD)
    far1, near2, dqt = run(*calls[1], dqt, None)
    moving = jnp.concatenate([moving, jnp.zeros_like(moving)])
    moving = send(add(near3, send(far3, CORE), moving), HOMEWARD)
    own_grad, near1, back = run(*calls[0], dqt, out)
    back = lax.all_to_all(back, "head", 0, 0, tiled=True)
    moving = send(add(near2, send(far2, CORE), moving), HOMEWARD)
    moving = send(add(near1, send(far1, CORE), moving), HOMEWARD)
    total = total32(own_grad, moving)
    sent = total.astype(BF16)
    total = total[0] + total32(*(send(sent[i], pairs) for i, pairs in ((1, TWIN), (2, CORE), (3, CROSS))))
    total = total.astype(BF16)
    back = jnp.transpose(back, (1, 2, 0, 3)).reshape(2, rows, GROUP * HEAD)
    return back[0], back[1], total[0], total[1]


def solution(mesh):
    spec = P(("inner", "outer"), "head")
    return jax.shard_map(
        on_device,
        mesh=mesh,
        in_specs=(spec, spec, spec, spec, P(), P()),
        out_specs=(spec, spec, spec, spec),
        check_vma=False,
    )
```

```python
import functools
import math

import jax
import jax.numpy as jnp
from jax import lax
from jax.experimental import pallas as pl
from jax.experimental.pallas import tpu as pltpu
from jax.sharding import PartitionSpec as P

HEAD = 128
GROUP = 8
BLOCK = 64
TILE = 4 * BLOCK
LANES = GROUP * BLOCK
CALL = 16
SCALE = 1.0 / math.sqrt(HEAD)
SCALE2 = SCALE * math.log2(math.e)
LOW = -1e30
NT = (((1,), (1,)), ((), ()))
TN = (((0,), (0,)), ((), ()))
NN = (((1,), (0,)), ((), ()))
F32, BF16 = jnp.float32, jnp.bfloat16


def mm(a, b, dims):
    return lax.dot_general(a, b, dims, preferred_element_type=F32)


def blocks_of(kinds, refs, meta):
    z, y, core = meta[0], meta[1] // 2, lax.rem(meta[1], 2)
    for (side, steps), ref in zip(kinds, refs, strict=True):
        sign = (1 - 2 * core) * (1 if side == "near" else -1)
        chunk = lax.rem(z - sign * steps + 8, 8)
        c = core if side == "near" else 1 - core
        first = lax.rem(y + c, 2) if steps else y
        for i in range(ref.shape[0]):
            shard = 2 * (first if i < 2 else 1 - first) + (c if i % 2 == 0 else 1 - c)
            for b in range(2):
                yield ref, i, b * BLOCK, chunk * 8 + shard * 2 + b


def limits(perm, meta, qb):
    lane = lax.rem(lax.broadcasted_iota(jnp.int32, (1, LANES), 1), BLOCK)
    block = perm[meta[0] * 8 + meta[1] * 2 + qb]
    first = block * BLOCK
    qpos = first + lane
    low = jnp.zeros_like(qpos)
    low_first = jnp.int32(0)
    for d in range(3):
        start = meta[2 + d]
        low = jnp.where(start <= qpos, jnp.maximum(low, start), low)
        low_first = jnp.where(start <= first, jnp.maximum(low_first, start), low_first)
    return qpos, low, low_first // BLOCK, block


def pick(perm, found, lowest, highest, k_s, v_s, pos_s, slot_s):
    n = jnp.int32(0)
    for i, (ref, shard, row, stored) in enumerate(found):
        at = pl.ds(pl.multiple_of(n * BLOCK, BLOCK), BLOCK)
        k_s[at, :] = ref[shard, 0, row : row + BLOCK, :]
        v_s[at, :] = ref[shard, 1, row : row + BLOCK, :]
        position = perm[stored]
        pos_s[n] = position
        slot_s[n] = i
        n = n + jnp.where((position >= lowest) & (position <= highest), 1, 0)
    for j in range(3):
        at = pl.ds(pl.multiple_of((n + j) * BLOCK, BLOCK), BLOCK)
        k_s[at, :] = jnp.zeros((BLOCK, HEAD), BF16)
        v_s[at, :] = jnp.zeros((BLOCK, HEAD), BF16)
        pos_s[n + j] = 1 << 14
        slot_s[n + j] = CALL
    return (n + 3) // 4


def tile(t):
    return pl.ds(pl.multiple_of(t * TILE, TILE), TILE)


def masked_scores(t, q, qpos, low, k_s, pos_s):
    row = lax.broadcasted_iota(jnp.int32, (BLOCK, 1), 0)
    kpos = jnp.concatenate([pos_s[4 * t + j] * BLOCK + row for j in range(4)], axis=0)
    return jnp.where((kpos <= qpos) & (kpos >= low), mm(k_s[tile(t), :], q, NT), LOW)


def heads_of(qd, which, qb):
    return jnp.concatenate([qd[i, which, qb * BLOCK : (qb + 1) * BLOCK, :] for i in range(GROUP)], axis=0)


def eights(x):
    return x.reshape(TILE // 8, 8, LANES)


def forward_kernel(kinds, first, last, *refs):
    perm, meta, qd, *refs = refs
    pieces, refs = refs[: len(kinds)], refs[len(kinds) :]
    if not first:
        stat_in, ot_in, *refs = refs
    stat, ot, k_s, v_s, s_s, pos_s, slot_s, *work = refs
    found = list(blocks_of(kinds, pieces, meta))
    for qb in range(2):
        q = heads_of(qd, 0, qb)
        qpos, low, lowest, highest = limits(perm, meta, qb)
        tiles = pick(perm, found, lowest, highest, k_s, v_s, pos_s, slot_s)

        def scores(t, top):
            s = masked_scores(t, q, qpos, low, k_s, pos_s)
            s_s[tile(t), :] = s
            return jnp.maximum(top, jnp.max(eights(s), axis=0))

        before = jnp.full((8, LANES), LOW, F32) if first else stat_in[qb, 0]
        top = lax.fori_loop(0, tiles, scores, before)
        top = jnp.max(top, axis=0, keepdims=True)
        acc = work[0] if last else ot.at[qb]
        if first:
            acc[...] = jnp.zeros((HEAD, LANES), F32)
            total = jnp.zeros((8, LANES), F32)
        else:
            keep = jnp.exp2((before[:1] - top) * SCALE2)
            acc[...] = ot_in[qb] * keep
            total = stat_in[qb, 1] * keep

        def sums(t, total):
            p = jnp.exp2((s_s[tile(t), :] - top) * SCALE2)
            acc[...] += mm(v_s[tile(t), :], p.astype(BF16), TN)
            return total + jnp.sum(eights(p), axis=0)

        total = lax.fori_loop(0, tiles, sums, total)
        if not last:
            stat[qb, 0] = jnp.broadcast_to(top, (8, LANES))
            stat[qb, 1] = total
            continue
        total = jnp.sum(total, axis=0, keepdims=True)
        out_t = acc[...] * (1.0 / total)
        out = out_t.T.astype(BF16)
        for i in range(GROUP):
            ot[i, qb * BLOCK : (qb + 1) * BLOCK, :] = out[i * BLOCK : (i + 1) * BLOCK, :]
        grad_t = heads_of(qd, 1, qb).astype(F32).T
        delta = jnp.sum(grad_t * out_t.astype(BF16).astype(F32), axis=0, keepdims=True)
        stat[qb, 0] = jnp.broadcast_to(top * SCALE2 + jnp.log2(total), (8, LANES))
        stat[qb, 1] = jnp.broadcast_to(delta, (8, LANES))


def backward_kernel(kinds, first, last, *refs):
    perm, meta, qd, stat, *refs = refs
    pieces, refs = refs[: len(kinds)], refs[len(kinds) :]
    if not first:
        dqt_in, *refs = refs
    if last:
        out, *refs = refs
    grads, refs = refs[: len(kinds)], refs[len(kinds) :]
    dq, k_s, v_s, dk_s, dv_s, pos_s, slot_s, *work = refs
    found = list(blocks_of(kinds, pieces, meta))
    dk_s[...] = jnp.zeros_like(dk_s)
    dv_s[...] = jnp.zeros_like(dv_s)
    for qb in range(2):
        q, do = heads_of(qd, 0, qb), heads_of(qd, 1, qb)
        qpos, low, lowest, highest = limits(perm, meta, qb)
        tiles = pick(perm, found, lowest, highest, k_s, v_s, pos_s, slot_s)
        lse, delta = stat[qb, 0, :1, :], stat[qb, 1, :1, :]
        acc = work[0] if last else dq.at[qb]
        acc[...] = jnp.zeros((HEAD, LANES), F32) if first else dqt_in[qb]

        def step(t, carry):
            p = jnp.exp2(masked_scores(t, q, qpos, low, k_s, pos_s) * SCALE2 - lse)
            dp = mm(v_s[tile(t), :], do, NT)
            ds = (p * (dp - delta)).astype(BF16)
            dv = mm(p.astype(BF16), do, NN)
            dk = mm(ds, q, NN)
            acc[...] += mm(k_s[tile(t), :], ds, TN)
            for j in range(4):
                at = pl.ds(pl.multiple_of(slot_s[4 * t + j] * BLOCK, BLOCK), BLOCK)
                dk_s[at, :] += dk[j * BLOCK : (j + 1) * BLOCK, :]
                dv_s[at, :] += dv[j * BLOCK : (j + 1) * BLOCK, :]
            return carry

        lax.fori_loop(0, tiles, step, 0)
        if last:
            done = (acc[...] * SCALE).T.astype(BF16)
            for i in range(GROUP):
                rows = slice(qb * BLOCK, (qb + 1) * BLOCK)
                dq[i, 0, rows, :] = out[i, rows, :]
                dq[i, 1, rows, :] = done[i * BLOCK : (i + 1) * BLOCK, :]
    n = 0
    for grad in grads:
        for i in range(grad.shape[0]):
            for b in range(2):
                at, rows = slice(n * BLOCK, (n + 1) * BLOCK), slice(b * BLOCK, (b + 1) * BLOCK)
                grad[i, 0, rows, :] = (dk_s[at, :] * SCALE).astype(BF16)
                grad[i, 1, rows, :] = dv_s[at, :].astype(BF16)
                n += 1


VMEM = pl.BlockSpec(memory_space=pltpu.VMEM)
SMEM = pl.BlockSpec(memory_space=pltpu.SMEM)
STAT = jax.ShapeDtypeStruct((2, 2, 8, LANES), F32)
WIDE = jax.ShapeDtypeStruct((2, HEAD, LANES), F32)
PICKED = [pltpu.VMEM(((CALL + 4) * BLOCK, HEAD), BF16)] * 2
LISTS = [pltpu.SMEM((CALL + 4,), jnp.int32)] * 2


def call(kernel, operands, outs, scratch, flops):
    return pl.pallas_call(
        kernel,
        out_shape=outs,
        in_specs=[SMEM, SMEM] + [VMEM] * (len(operands) - 2),
        out_specs=[VMEM] * len(outs),
        scratch_shapes=scratch,
        compiler_params=pltpu.CompilerParams(vmem_limit_bytes=20 * 1024 * 1024),
        cost_estimate=pl.CostEstimate(flops=flops, bytes_accessed=2 * 10**6, transcendentals=10**6),
    )(*operands)


def forward(perm, meta, qd, kinds, pieces, state, last):
    first = state is None
    outs = [STAT, jax.ShapeDtypeStruct((GROUP, 128, HEAD), BF16) if last else WIDE]
    scratch = PICKED + [pltpu.VMEM(((CALL + 4) * BLOCK, LANES), F32)] + LISTS
    scratch += [pltpu.VMEM((HEAD, LANES), F32)] if last else []
    kernel = functools.partial(forward_kernel, kinds, first, last)
    return call(kernel, [perm, meta, qd, *pieces, *(state or [])], outs, scratch, 5 * 10**8)


def backward(perm, meta, qd, stat, kinds, pieces, dqt, out):
    first, last = dqt is None, out is not None
    outs = [jax.ShapeDtypeStruct(p.shape, BF16) for p in pieces]
    outs.append(jax.ShapeDtypeStruct((GROUP, 2, 128, HEAD), BF16) if last else WIDE)
    scratch = PICKED + [pltpu.VMEM(((CALL + 1) * BLOCK, HEAD), F32)] * 2 + LISTS
    scratch += [pltpu.VMEM((HEAD, LANES), F32)] if last else []
    operands = [perm, meta, qd, stat, *pieces] + ([] if first else [dqt]) + ([out] if last else [])
    return call(functools.partial(backward_kernel, kinds, first, last), operands, outs, scratch, 10**9)


def outer_perm(move):
    pairs = []
    for z in range(8):
        for y in range(2):
            for c in range(2):
                z2, y2, c2 = move(z, y, c)
                pairs.append((z * 4 + y * 2 + c, (z2 % 8) * 4 + y2 * 2 + c2))
    return pairs


AXES = ("inner", "outer")
CORE = outer_perm(lambda z, y, c: (z, y, 1 - c))
TWIN = outer_perm(lambda z, y, c: (z, 1 - y, c))
ONWARD = outer_perm(lambda z, y, c: (z + 1 - 2 * c, y, c))
HOMEWARD = outer_perm(lambda z, y, c: (z - 1 + 2 * c, y, c))
FIRST_ON = [outer_perm(lambda z, y, c, n=n: (z + 1 - 2 * c, (y + c + n) % 2, c)) for n in range(2)]
LAST_HOME = [outer_perm(lambda z, y, c, n=n: (z - 1 + 2 * c, (y + c + n) % 2, c)) for n in range(2)]


def send(x, pairs):
    return lax.ppermute(x, AXES, pairs)


def after(*values):
    return lax.optimization_barrier(values)


def total32(*terms):
    return sum(t.astype(F32) for t in terms)


def add(*terms):
    return total32(*terms).astype(BF16)


def on_device(queries, keys, values, output_gradient, block_perm, segment_ids):
    rows = queries.shape[0]
    kv = jnp.stack([keys, values])
    pair = jnp.stack([kv, send(kv, CORE)])
    near1 = jnp.concatenate([send(pair, pairs) for pairs in FIRST_ON])
    own = jnp.concatenate([pair, send(pair, TWIN)])
    qd = jnp.stack([queries.reshape(rows, GROUP, HEAD), output_gradient.reshape(rows, GROUP, HEAD)])
    qd = lax.all_to_all(jnp.transpose(qd, (2, 0, 1, 3)), "head", 0, 0, tiled=True)
    starts = jnp.sum(segment_ids[None, :] < jnp.arange(1, 4, dtype=jnp.int32)[:, None], axis=1)
    place = jnp.stack([lax.axis_index("inner"), lax.axis_index("outer")])
    meta = jnp.concatenate([place.astype(jnp.int32), starts.astype(jnp.int32)])

    run = functools.partial(forward, block_perm, meta, qd)
    near2 = send(near1, ONWARD)
    near3 = send(near2, ONWARD)
    state = run((("near", 1), ("near", 2)), (near1, near2), None, False)
    near3, near1, near2, *state = after(near3, near1, near2, *state)
    near4 = send(near3, ONWARD)
    far1, far2, far3 = (send(x, CORE) for x in (near1, near2, near3))
    state = run((("near", 3), ("near", 0)), (near3, own), state, False)
    state = run((("far", 1), ("far", 2)), (far1, far2), state, False)
    near4, *state = after(near4, *state)
    stat, out = run((("far", 3), ("near", 4)), (far3, near4), state, True)

    run = functools.partial(backward, block_perm, meta, qd, stat)
    far3, near4, dqt = run((("far", 3), ("near", 4)), (far3, near4), None, None)
    moving = send(near4, HOMEWARD)
    far3 = send(far3, CORE)
    near3, far2, dqt = run((("near", 3), ("far", 2)), (near3, far2), dqt, None)
    near2, far1, dqt = run((("near", 2), ("far", 1)), (near2, far1), dqt, None)
    moving, far2, dqt = after(moving, far2, dqt)
    moving = send(add(near3, far3, moving), HOMEWARD)
    far2 = send(far2, CORE)
    near1, own, back = run((("near", 1), ("near", 0)), (near1, own), dqt, out)
    moving, far1, own, back = after(moving, far1, own, back)
    moving = send(add(near2, far2, moving), HOMEWARD)
    far1 = send(far1, CORE)
    own_twin = send(own[2:], TWIN)
    back = lax.all_to_all(back, "head", 0, 0, tiled=True)
    moving = add(near1, far1, moving)
    pair = total32(own[:2], own_twin, *(send(moving[2 * n : 2 * n + 2], LAST_HOME[n]) for n in range(2)))
    back = jnp.transpose(back, (1, 2, 0, 3)).reshape(2, rows, GROUP * HEAD)
    pair, attended, query_grad = after(pair, back[0], back[1])
    total = add(pair[0], send(pair[1].astype(BF16), CORE))
    return attended, query_grad, total[0], total[1]


def solution(mesh):
    spec = P(("inner", "outer"), "head")
    return jax.shard_map(
        on_device,
        mesh=mesh,
        in_specs=(spec, spec, spec, spec, P(), P()),
        out_specs=(spec, spec, spec, spec),
        check_vma=False,
    )
```

```python
import functools
import math

import jax
import jax.numpy as jnp
from jax import lax
from jax.experimental import pallas as pl
from jax.experimental.pallas import tpu as pltpu
from jax.sharding import PartitionSpec as P

HEAD = 128
GROUP = 8
BLOCK = 64
TILE = 4 * BLOCK
LANES = GROUP * BLOCK
CALL = 16
SCALE = 1.0 / math.sqrt(HEAD)
SCALE2 = SCALE * math.log2(math.e)
LOW = -1e30
NT = (((1,), (1,)), ((), ()))
TN = (((0,), (0,)), ((), ()))
NN = (((1,), (0,)), ((), ()))
F32, BF16 = jnp.float32, jnp.bfloat16


def mm(a, b, dims):
    return lax.dot_general(a, b, dims, preferred_element_type=F32)


def blocks_of(kinds, refs, meta):
    z, y, core = meta[0], meta[1] // 2, lax.rem(meta[1], 2)
    for (side, steps), ref in zip(kinds, refs, strict=True):
        sign = (1 - 2 * core) * (1 if side == "near" else -1)
        chunk = lax.rem(z - sign * steps + 8, 8)
        c = core if side == "near" else 1 - core
        first = lax.rem(y + c, 2) if steps else y
        for i in range(ref.shape[0]):
            shard = 2 * (first if i < 2 else 1 - first) + (c if i % 2 == 0 else 1 - c)
            for b in range(2):
                yield ref, i, b * BLOCK, chunk * 8 + shard * 2 + b


def limits(perm, meta, qb):
    lane = lax.rem(lax.broadcasted_iota(jnp.int32, (1, LANES), 1), BLOCK)
    block = perm[meta[0] * 8 + meta[1] * 2 + qb]
    first = block * BLOCK
    qpos = first + lane
    low = jnp.zeros_like(qpos)
    low_first = jnp.int32(0)
    for d in range(3):
        start = meta[2 + d]
        low = jnp.where(start <= qpos, jnp.maximum(low, start), low)
        low_first = jnp.where(start <= first, jnp.maximum(low_first, start), low_first)
    return qpos, low, low_first // BLOCK, block


def pick(perm, found, lowest, highest, k_s, v_s, pos_s, slot_s):
    n = jnp.int32(0)
    for i, (ref, shard, row, stored) in enumerate(found):
        at = pl.ds(pl.multiple_of(n * BLOCK, BLOCK), BLOCK)
        k_s[at, :] = ref[shard, 0, row : row + BLOCK, :]
        v_s[at, :] = ref[shard, 1, row : row + BLOCK, :]
        position = perm[stored]
        pos_s[n] = position
        slot_s[n] = i
        n = n + jnp.where((position >= lowest) & (position <= highest), 1, 0)
    for j in range(3):
        at = pl.ds(pl.multiple_of((n + j) * BLOCK, BLOCK), BLOCK)
        k_s[at, :] = jnp.zeros((BLOCK, HEAD), BF16)
        v_s[at, :] = jnp.zeros((BLOCK, HEAD), BF16)
        pos_s[n + j] = 1 << 14
        slot_s[n + j] = CALL
    return (n + 3) // 4


def tile(t):
    return pl.ds(pl.multiple_of(t * TILE, TILE), TILE)


def masked_scores(t, q, qpos, low, k_s, pos_s):
    row = lax.broadcasted_iota(jnp.int32, (BLOCK, 1), 0)
    kpos = jnp.concatenate([pos_s[4 * t + j] * BLOCK + row for j in range(4)], axis=0)
    return jnp.where((kpos <= qpos) & (kpos >= low), mm(k_s[tile(t), :], q, NT), LOW)


def heads_of(qd, which, qb):
    return jnp.concatenate([qd[i, which, qb * BLOCK : (qb + 1) * BLOCK, :] for i in range(GROUP)], axis=0)


def eights(x):
    return x.reshape(TILE // 8, 8, LANES)


def forward_kernel(kinds, first, last, *refs):
    perm, meta, qd, *refs = refs
    pieces, refs = refs[: len(kinds)], refs[len(kinds) :]
    if not first:
        stat_in, ot_in, *refs = refs
    stat, ot, k_s, v_s, s_s, pos_s, slot_s, *work = refs
    found = list(blocks_of(kinds, pieces, meta))
    for qb in range(2):
        q = heads_of(qd, 0, qb)
        qpos, low, lowest, highest = limits(perm, meta, qb)
        tiles = pick(perm, found, lowest, highest, k_s, v_s, pos_s, slot_s)

        def scores(t, top):
            s = masked_scores(t, q, qpos, low, k_s, pos_s)
            s_s[tile(t), :] = s
            return jnp.maximum(top, jnp.max(eights(s), axis=0))

        before = jnp.full((8, LANES), LOW, F32) if first else stat_in[qb, 0]
        top = lax.fori_loop(0, tiles, scores, before)
        top = jnp.max(top, axis=0, keepdims=True)
        acc = work[0] if last else ot.at[qb]
        if first:
            acc[...] = jnp.zeros((HEAD, LANES), F32)
            total = jnp.zeros((8, LANES), F32)
        else:
            keep = jnp.exp2((before[:1] - top) * SCALE2)
            acc[...] = ot_in[qb] * keep
            total = stat_in[qb, 1] * keep

        def sums(t, total):
            p = jnp.exp2((s_s[tile(t), :] - top) * SCALE2)
            acc[...] += mm(v_s[tile(t), :], p.astype(BF16), TN)
            return total + jnp.sum(eights(p), axis=0)

        total = lax.fori_loop(0, tiles, sums, total)
        if not last:
            stat[qb, 0] = jnp.broadcast_to(top, (8, LANES))
            stat[qb, 1] = total
            continue
        total = jnp.sum(total, axis=0, keepdims=True)
        out_t = acc[...] * (1.0 / total)
        out = out_t.T.astype(BF16)
        for i in range(GROUP):
            ot[i, qb * BLOCK : (qb + 1) * BLOCK, :] = out[i * BLOCK : (i + 1) * BLOCK, :]
        grad_t = heads_of(qd, 1, qb).astype(F32).T
        delta = jnp.sum(grad_t * out_t.astype(BF16).astype(F32), axis=0, keepdims=True)
        stat[qb, 0] = jnp.broadcast_to(top * SCALE2 + jnp.log2(total), (8, LANES))
        stat[qb, 1] = jnp.broadcast_to(delta, (8, LANES))


def backward_kernel(kinds, first, last, *refs):
    perm, meta, qd, stat, *refs = refs
    pieces, refs = refs[: len(kinds)], refs[len(kinds) :]
    if not first:
        dqt_in, *refs = refs
    if last:
        out, *refs = refs
    grads, refs = refs[: len(kinds)], refs[len(kinds) :]
    dq, k_s, v_s, dk_s, dv_s, pos_s, slot_s, *work = refs
    found = list(blocks_of(kinds, pieces, meta))
    dk_s[...] = jnp.zeros_like(dk_s)
    dv_s[...] = jnp.zeros_like(dv_s)
    for qb in range(2):
        q, do = heads_of(qd, 0, qb), heads_of(qd, 1, qb)
        qpos, low, lowest, highest = limits(perm, meta, qb)
        tiles = pick(perm, found, lowest, highest, k_s, v_s, pos_s, slot_s)
        lse, delta = stat[qb, 0, :1, :], stat[qb, 1, :1, :]
        acc = work[0] if last else dq.at[qb]
        acc[...] = jnp.zeros((HEAD, LANES), F32) if first else dqt_in[qb]

        def step(t, carry):
            p = jnp.exp2(masked_scores(t, q, qpos, low, k_s, pos_s) * SCALE2 - lse)
            dp = mm(v_s[tile(t), :], do, NT)
            ds = (p * (dp - delta)).astype(BF16)
            dv = mm(p.astype(BF16), do, NN)
            dk = mm(ds, q, NN)
            acc[...] += mm(k_s[tile(t), :], ds, TN)
            for j in range(4):
                at = pl.ds(pl.multiple_of(slot_s[4 * t + j] * BLOCK, BLOCK), BLOCK)
                dk_s[at, :] += dk[j * BLOCK : (j + 1) * BLOCK, :]
                dv_s[at, :] += dv[j * BLOCK : (j + 1) * BLOCK, :]
            return carry

        lax.fori_loop(0, tiles, step, 0)
        if last:
            done = (acc[...] * SCALE).T.astype(BF16)
            for i in range(GROUP):
                rows = slice(qb * BLOCK, (qb + 1) * BLOCK)
                dq[i, 0, rows, :] = out[i, rows, :]
                dq[i, 1, rows, :] = done[i * BLOCK : (i + 1) * BLOCK, :]
    n = 0
    for grad in grads:
        for i in range(grad.shape[0]):
            for b in range(2):
                at, rows = slice(n * BLOCK, (n + 1) * BLOCK), slice(b * BLOCK, (b + 1) * BLOCK)
                grad[i, 0, rows, :] = (dk_s[at, :] * SCALE).astype(BF16)
                grad[i, 1, rows, :] = dv_s[at, :].astype(BF16)
                n += 1


VMEM = pl.BlockSpec(memory_space=pltpu.VMEM)
SMEM = pl.BlockSpec(memory_space=pltpu.SMEM)
STAT = jax.ShapeDtypeStruct((2, 2, 8, LANES), F32)
WIDE = jax.ShapeDtypeStruct((2, HEAD, LANES), F32)
PICKED = [pltpu.VMEM(((CALL + 4) * BLOCK, HEAD), BF16)] * 2
LISTS = [pltpu.SMEM((CALL + 4,), jnp.int32)] * 2


def call(kernel, operands, outs, scratch, flops):
    return pl.pallas_call(
        kernel,
        out_shape=outs,
        in_specs=[SMEM, SMEM] + [VMEM] * (len(operands) - 2),
        out_specs=[VMEM] * len(outs),
        scratch_shapes=scratch,
        compiler_params=pltpu.CompilerParams(vmem_limit_bytes=20 * 1024 * 1024),
        cost_estimate=pl.CostEstimate(flops=flops, bytes_accessed=2 * 10**6, transcendentals=10**6),
    )(*operands)


def forward(perm, meta, qd, kinds, pieces, state, last):
    first = state is None
    outs = [STAT, jax.ShapeDtypeStruct((GROUP, 128, HEAD), BF16) if last else WIDE]
    scratch = PICKED + [pltpu.VMEM(((CALL + 4) * BLOCK, LANES), F32)] + LISTS
    scratch += [pltpu.VMEM((HEAD, LANES), F32)] if last else []
    kernel = functools.partial(forward_kernel, kinds, first, last)
    return call(kernel, [perm, meta, qd, *pieces, *(state or [])], outs, scratch, 5 * 10**8)


def backward(perm, meta, qd, stat, kinds, pieces, dqt, out):
    first, last = dqt is None, out is not None
    outs = [jax.ShapeDtypeStruct(p.shape, BF16) for p in pieces]
    outs.append(jax.ShapeDtypeStruct((GROUP, 2, 128, HEAD), BF16) if last else WIDE)
    scratch = PICKED + [pltpu.VMEM(((CALL + 1) * BLOCK, HEAD), F32)] * 2 + LISTS
    scratch += [pltpu.VMEM((HEAD, LANES), F32)] if last else []
    operands = [perm, meta, qd, stat, *pieces] + ([] if first else [dqt]) + ([out] if last else [])
    return call(functools.partial(backward_kernel, kinds, first, last), operands, outs, scratch, 10**9)


def outer_perm(move):
    pairs = []
    for z in range(8):
        for y in range(2):
            for c in range(2):
                z2, y2, c2 = move(z, y, c)
                pairs.append((z * 4 + y * 2 + c, (z2 % 8) * 4 + y2 * 2 + c2))
    return pairs


AXES = ("inner", "outer")
CORE = outer_perm(lambda z, y, c: (z, y, 1 - c))
TWIN = outer_perm(lambda z, y, c: (z, 1 - y, c))
ONWARD = outer_perm(lambda z, y, c: (z + 1 - 2 * c, y, c))
HOMEWARD = outer_perm(lambda z, y, c: (z - 1 + 2 * c, y, c))
FIRST_ON = [outer_perm(lambda z, y, c, n=n: (z + 1 - 2 * c, (y + c + n) % 2, c)) for n in range(2)]
LAST_HOME = [outer_perm(lambda z, y, c, n=n: (z - 1 + 2 * c, (y + c + n) % 2, c)) for n in range(2)]


def send(x, pairs):
    return lax.ppermute(x, AXES, pairs)


def after(*values):
    return lax.optimization_barrier(values)


def total32(*terms):
    return sum(t.astype(F32) for t in terms)


def add(*terms):
    return total32(*terms).astype(BF16)


def on_device(queries, keys, values, output_gradient, block_perm, segment_ids):
    rows = queries.shape[0]
    kv = jnp.stack([keys, values])
    pair = jnp.stack([kv, send(kv, CORE)])
    near1 = jnp.concatenate([send(pair, pairs) for pairs in FIRST_ON])
    own = jnp.concatenate([pair, send(pair, TWIN)])
    qd = jnp.stack([queries.reshape(rows, GROUP, HEAD), output_gradient.reshape(rows, GROUP, HEAD)])
    qd = lax.all_to_all(jnp.transpose(qd, (2, 0, 1, 3)), "head", 0, 0, tiled=True)
    segment_ids, qd = after(segment_ids, qd)
    starts = jnp.sum(segment_ids[None, :] < jnp.arange(1, 4, dtype=jnp.int32)[:, None], axis=1)
    place = jnp.stack([lax.axis_index("inner"), lax.axis_index("outer")])
    meta = jnp.concatenate([place.astype(jnp.int32), starts.astype(jnp.int32)])

    near2 = send(near1, ONWARD)
    near3 = send(near2, ONWARD)
    run = functools.partial(forward, block_perm, meta, qd)
    state = run((("near", 1), ("near", 2)), (near1, near2), None, False)
    near3, near1, near2, *state = after(near3, near1, near2, *state)
    near4 = send(near3, ONWARD)
    far1, far2, far3 = (send(x, CORE) for x in (near1, near2, near3))
    state = run((("near", 3), ("near", 0)), (near3, own), state, False)
    state = run((("far", 1), ("far", 2)), (far1, far2), state, False)
    near4, *state = after(near4, *state)
    stat, out = run((("far", 3), ("near", 4)), (far3, near4), state, True)

    run = functools.partial(backward, block_perm, meta, qd, stat)
    far3, near4, dqt = run((("far", 3), ("near", 4)), (far3, near4), None, None)
    moving = send(near4, HOMEWARD)
    far3 = send(far3, CORE)
    near3, far2, dqt = run((("near", 3), ("far", 2)), (near3, far2), dqt, None)
    near2, far1, dqt = run((("near", 2), ("far", 1)), (near2, far1), dqt, None)
    moving, far2, dqt = after(moving, far2, dqt)
    moving = send(add(near3, far3, moving), HOMEWARD)
    far2 = send(far2, CORE)
    near1, own, back = run((("near", 1), ("near", 0)), (near1, own), dqt, out)
    moving, far1, own, back = after(moving, far1, own, back)
    moving = send(add(near2, far2, moving), HOMEWARD)
    far1 = send(far1, CORE)
    own_twin = send(own[2:], TWIN)
    back = lax.all_to_all(back, "head", 0, 0, tiled=True)
    moving = add(near1, far1, moving)
    pair = total32(own[:2], own_twin, *(send(moving[2 * n : 2 * n + 2], LAST_HOME[n]) for n in range(2)))
    back = jnp.transpose(back, (1, 2, 0, 3)).reshape(2, rows, GROUP * HEAD)
    pair, attended, query_grad = after(pair, back[0], back[1])
    total = add(pair[0], send(pair[1].astype(BF16), CORE))
    return attended, query_grad, total[0], total[1]


def solution(mesh):
    spec = P(("inner", "outer"), "head")
    return jax.shard_map(
        on_device,
        mesh=mesh,
        in_specs=(spec, spec, spec, spec, P(), P()),
        out_specs=(spec, spec, spec, spec),
        check_vma=False,
    )
```

```python
import functools
import math

import jax
import jax.numpy as jnp
from jax import lax
from jax.experimental import pallas as pl
from jax.experimental.pallas import tpu as pltpu
from jax.sharding import PartitionSpec as P

HEAD = 128
GROUP = 8
BLOCK = 64
TILE = 4 * BLOCK
LANES = GROUP * BLOCK
CALL = 16
SCALE = 1.0 / math.sqrt(HEAD)
SCALE2 = SCALE * math.log2(math.e)
LOW = -1e30
NT = (((1,), (1,)), ((), ()))
TN = (((0,), (0,)), ((), ()))
NN = (((1,), (0,)), ((), ()))
F32, BF16 = jnp.float32, jnp.bfloat16


def mm(a, b, dims):
    return lax.dot_general(a, b, dims, preferred_element_type=F32)


def blocks_of(kinds, refs, meta):
    z, y, core = meta[0], meta[1] // 2, lax.rem(meta[1], 2)
    for (side, steps), ref in zip(kinds, refs, strict=True):
        sign = (1 - 2 * core) * (1 if side == "near" else -1)
        chunk = lax.rem(z - sign * steps + 8, 8)
        c = core if side == "near" else 1 - core
        first = lax.rem(y + c, 2) if steps else y
        for i in range(ref.shape[0]):
            shard = 2 * (first if i < 2 else 1 - first) + (c if i % 2 == 0 else 1 - c)
            for b in range(2):
                yield ref, i, b * BLOCK, chunk * 8 + shard * 2 + b


def limits(perm, meta, qb):
    lane = lax.rem(lax.broadcasted_iota(jnp.int32, (1, LANES), 1), BLOCK)
    block = perm[meta[0] * 8 + meta[1] * 2 + qb]
    first = block * BLOCK
    qpos = first + lane
    low = jnp.zeros_like(qpos)
    low_first = jnp.int32(0)
    for d in range(3):
        start = meta[2 + d]
        low = jnp.where(start <= qpos, jnp.maximum(low, start), low)
        low_first = jnp.where(start <= first, jnp.maximum(low_first, start), low_first)
    return qpos, low, low_first // BLOCK, block


def pick(perm, found, lowest, highest, k_s, v_s, pos_s, slot_s):
    n = jnp.int32(0)
    for i, (ref, shard, row, stored) in enumerate(found):
        at = pl.ds(pl.multiple_of(n * BLOCK, BLOCK), BLOCK)
        k_s[at, :] = ref[shard, 0, row : row + BLOCK, :]
        v_s[at, :] = ref[shard, 1, row : row + BLOCK, :]
        position = perm[stored]
        pos_s[n] = position
        slot_s[n] = i
        n = n + jnp.where((position >= lowest) & (position <= highest), 1, 0)
    for j in range(3):
        at = pl.ds(pl.multiple_of((n + j) * BLOCK, BLOCK), BLOCK)
        k_s[at, :] = jnp.zeros((BLOCK, HEAD), BF16)
        v_s[at, :] = jnp.zeros((BLOCK, HEAD), BF16)
        pos_s[n + j] = 1 << 14
        slot_s[n + j] = CALL
    return (n + 3) // 4


def tile(t):
    return pl.ds(pl.multiple_of(t * TILE, TILE), TILE)


def masked_scores(t, q, qpos, low, k_s, pos_s):
    row = lax.broadcasted_iota(jnp.int32, (BLOCK, 1), 0)
    kpos = jnp.concatenate([pos_s[4 * t + j] * BLOCK + row for j in range(4)], axis=0)
    return jnp.where((kpos <= qpos) & (kpos >= low), mm(k_s[tile(t), :], q, NT), LOW)


def heads_of(qd, which, qb):
    return jnp.concatenate([qd[i, which, qb * BLOCK : (qb + 1) * BLOCK, :] for i in range(GROUP)], axis=0)


def eights(x):
    return x.reshape(TILE // 8, 8, LANES)


def forward_kernel(kinds, first, last, *refs):
    perm, meta, qd, *refs = refs
    pieces, refs = refs[: len(kinds)], refs[len(kinds) :]
    if not first:
        stat_in, ot_in, *refs = refs
    stat, ot, k_s, v_s, s_s, pos_s, slot_s, *work = refs
    found = list(blocks_of(kinds, pieces, meta))
    for qb in range(2):
        q = heads_of(qd, 0, qb)
        qpos, low, lowest, highest = limits(perm, meta, qb)
        tiles = pick(perm, found, lowest, highest, k_s, v_s, pos_s, slot_s)

        def scores(t, top):
            s = masked_scores(t, q, qpos, low, k_s, pos_s)
            s_s[tile(t), :] = s
            return jnp.maximum(top, jnp.max(eights(s), axis=0))

        before = jnp.full((8, LANES), LOW, F32) if first else stat_in[qb, 0]
        top = lax.fori_loop(0, tiles, scores, before)
        top = jnp.max(top, axis=0, keepdims=True)
        acc = work[0] if last else ot.at[qb]
        if first:
            acc[...] = jnp.zeros((HEAD, LANES), F32)
            total = jnp.zeros((8, LANES), F32)
        else:
            keep = jnp.exp2((before[:1] - top) * SCALE2)
            acc[...] = ot_in[qb] * keep
            total = stat_in[qb, 1] * keep

        def sums(t, total):
            p = jnp.exp2((s_s[tile(t), :] - top) * SCALE2)
            acc[...] += mm(v_s[tile(t), :], p.astype(BF16), TN)
            return total + jnp.sum(eights(p), axis=0)

        total = lax.fori_loop(0, tiles, sums, total)
        if not last:
            stat[qb, 0] = jnp.broadcast_to(top, (8, LANES))
            stat[qb, 1] = total
            continue
        total = jnp.sum(total, axis=0, keepdims=True)
        out_t = acc[...] * (1.0 / total)
        out = out_t.T.astype(BF16)
        for i in range(GROUP):
            ot[i, qb * BLOCK : (qb + 1) * BLOCK, :] = out[i * BLOCK : (i + 1) * BLOCK, :]
        grad_t = heads_of(qd, 1, qb).astype(F32).T
        delta = jnp.sum(grad_t * out_t.astype(BF16).astype(F32), axis=0, keepdims=True)
        stat[qb, 0] = jnp.broadcast_to(top * SCALE2 + jnp.log2(total), (8, LANES))
        stat[qb, 1] = jnp.broadcast_to(delta, (8, LANES))


def backward_kernel(kinds, first, last, *refs):
    perm, meta, qd, stat, *refs = refs
    pieces, refs = refs[: len(kinds)], refs[len(kinds) :]
    if not first:
        dqt_in, *refs = refs
    if last:
        out, *refs = refs
    grads, refs = refs[: len(kinds)], refs[len(kinds) :]
    dq, k_s, v_s, dk_s, dv_s, pos_s, slot_s, *work = refs
    found = list(blocks_of(kinds, pieces, meta))
    dk_s[...] = jnp.zeros_like(dk_s)
    dv_s[...] = jnp.zeros_like(dv_s)
    for qb in range(2):
        q, do = heads_of(qd, 0, qb), heads_of(qd, 1, qb)
        qpos, low, lowest, highest = limits(perm, meta, qb)
        tiles = pick(perm, found, lowest, highest, k_s, v_s, pos_s, slot_s)
        lse, delta = stat[qb, 0, :1, :], stat[qb, 1, :1, :]
        acc = work[0] if last else dq.at[qb]
        acc[...] = jnp.zeros((HEAD, LANES), F32) if first else dqt_in[qb]

        def step(t, carry):
            p = jnp.exp2(masked_scores(t, q, qpos, low, k_s, pos_s) * SCALE2 - lse)
            dp = mm(v_s[tile(t), :], do, NT)
            ds = (p * (dp - delta)).astype(BF16)
            dv = mm(p.astype(BF16), do, NN)
            dk = mm(ds, q, NN)
            acc[...] += mm(k_s[tile(t), :], ds, TN)
            for j in range(4):
                at = pl.ds(pl.multiple_of(slot_s[4 * t + j] * BLOCK, BLOCK), BLOCK)
                dk_s[at, :] += dk[j * BLOCK : (j + 1) * BLOCK, :]
                dv_s[at, :] += dv[j * BLOCK : (j + 1) * BLOCK, :]
            return carry

        lax.fori_loop(0, tiles, step, 0)
        if last:
            done = (acc[...] * SCALE).T.astype(BF16)
            for i in range(GROUP):
                rows = slice(qb * BLOCK, (qb + 1) * BLOCK)
                dq[i, 0, rows, :] = out[i, rows, :]
                dq[i, 1, rows, :] = done[i * BLOCK : (i + 1) * BLOCK, :]
    n = 0
    for grad in grads:
        for i in range(grad.shape[0]):
            for b in range(2):
                at, rows = slice(n * BLOCK, (n + 1) * BLOCK), slice(b * BLOCK, (b + 1) * BLOCK)
                grad[i, 0, rows, :] = (dk_s[at, :] * SCALE).astype(BF16)
                grad[i, 1, rows, :] = dv_s[at, :].astype(BF16)
                n += 1


VMEM = pl.BlockSpec(memory_space=pltpu.VMEM)
SMEM = pl.BlockSpec(memory_space=pltpu.SMEM)
STAT = jax.ShapeDtypeStruct((2, 2, 8, LANES), F32)
WIDE = jax.ShapeDtypeStruct((2, HEAD, LANES), F32)
PICKED = [pltpu.VMEM(((CALL + 4) * BLOCK, HEAD), BF16)] * 2
LISTS = [pltpu.SMEM((CALL + 4,), jnp.int32)] * 2


def call(kernel, operands, outs, scratch, flops):
    return pl.pallas_call(
        kernel,
        out_shape=outs,
        in_specs=[SMEM, SMEM] + [VMEM] * (len(operands) - 2),
        out_specs=[VMEM] * len(outs),
        scratch_shapes=scratch,
        compiler_params=pltpu.CompilerParams(vmem_limit_bytes=20 * 1024 * 1024),
        cost_estimate=pl.CostEstimate(flops=flops, bytes_accessed=2 * 10**6, transcendentals=10**6),
    )(*operands)


def forward(perm, meta, qd, kinds, pieces, state, last):
    first = state is None
    outs = [STAT, jax.ShapeDtypeStruct((GROUP, 128, HEAD), BF16) if last else WIDE]
    scratch = PICKED + [pltpu.VMEM(((CALL + 4) * BLOCK, LANES), F32)] + LISTS
    scratch += [pltpu.VMEM((HEAD, LANES), F32)] if last else []
    kernel = functools.partial(forward_kernel, kinds, first, last)
    return call(kernel, [perm, meta, qd, *pieces, *(state or [])], outs, scratch, 5 * 10**8)


def backward(perm, meta, qd, stat, kinds, pieces, dqt, out):
    first, last = dqt is None, out is not None
    outs = [jax.ShapeDtypeStruct(p.shape, BF16) for p in pieces]
    outs.append(jax.ShapeDtypeStruct((GROUP, 2, 128, HEAD), BF16) if last else WIDE)
    scratch = PICKED + [pltpu.VMEM(((CALL + 1) * BLOCK, HEAD), F32)] * 2 + LISTS
    scratch += [pltpu.VMEM((HEAD, LANES), F32)] if last else []
    operands = [perm, meta, qd, stat, *pieces] + ([] if first else [dqt]) + ([out] if last else [])
    return call(functools.partial(backward_kernel, kinds, first, last), operands, outs, scratch, 10**9)


def split_heads(q, do, both):
    for i in range(GROUP):
        both[i, 0] = q[:, i * HEAD : (i + 1) * HEAD]
        both[i, 1] = do[:, i * HEAD : (i + 1) * HEAD]


def join_heads(both, out, dq):
    for i in range(GROUP):
        out[:, i * HEAD : (i + 1) * HEAD] = both[i, 0]
        dq[:, i * HEAD : (i + 1) * HEAD] = both[i, 1]


def relayout(kernel, operands, outs):
    return pl.pallas_call(
        kernel,
        out_shape=[jax.ShapeDtypeStruct(shape, BF16) for shape in outs],
        in_specs=[VMEM] * len(operands),
        out_specs=[VMEM] * len(outs),
        cost_estimate=pl.CostEstimate(flops=0, bytes_accessed=10**6, transcendentals=0),
    )(*operands)


def outer_perm(move):
    pairs = []
    for z in range(8):
        for y in range(2):
            for c in range(2):
                z2, y2, c2 = move(z, y, c)
                pairs.append((z * 4 + y * 2 + c, (z2 % 8) * 4 + y2 * 2 + c2))
    return pairs


AXES = ("inner", "outer")
CORE = outer_perm(lambda z, y, c: (z, y, 1 - c))
TWIN = outer_perm(lambda z, y, c: (z, 1 - y, c))
ONWARD = outer_perm(lambda z, y, c: (z + 1 - 2 * c, y, c))
HOMEWARD = outer_perm(lambda z, y, c: (z - 1 + 2 * c, y, c))
FIRST_ON = [outer_perm(lambda z, y, c, n=n: (z + 1 - 2 * c, (y + c + n) % 2, c)) for n in range(2)]
LAST_HOME = [outer_perm(lambda z, y, c, n=n: (z - 1 + 2 * c, (y + c + n) % 2, c)) for n in range(2)]


def send(x, pairs):
    return lax.ppermute(x, AXES, pairs)


def after(*values):
    return lax.optimization_barrier(values)


def total32(*terms):
    return sum(t.astype(F32) for t in terms)


def add(*terms):
    return total32(*terms).astype(BF16)


def on_device(queries, keys, values, output_gradient, block_perm, segment_ids):
    rows = queries.shape[0]
    kv = jnp.stack([keys, values])
    pair = jnp.stack([kv, send(kv, CORE)])
    near1 = jnp.concatenate([send(pair, pairs) for pairs in FIRST_ON])
    own = jnp.concatenate([pair, send(pair, TWIN)])
    (qd,) = relayout(split_heads, [queries, output_gradient], [(GROUP, 2, rows, HEAD)])
    qd = lax.all_to_all(qd, "head", 0, 0, tiled=True)
    segment_ids, qd = after(segment_ids, qd)
    starts = jnp.sum(segment_ids[None, :] < jnp.arange(1, 4, dtype=jnp.int32)[:, None], axis=1)
    place = jnp.stack([lax.axis_index("inner"), lax.axis_index("outer")])
    meta = jnp.concatenate([place.astype(jnp.int32), starts.astype(jnp.int32)])

    near2 = send(near1, ONWARD)
    near3 = send(near2, ONWARD)
    run = functools.partial(forward, block_perm, meta, qd)
    state = run((("near", 1), ("near", 2)), (near1, near2), None, False)
    near3, near1, near2, *state = after(near3, near1, near2, *state)
    near4 = send(near3, ONWARD)
    far1, far2, far3 = (send(x, CORE) for x in (near1, near2, near3))
    state = run((("near", 3), ("near", 0)), (near3, own), state, False)
    state = run((("far", 1), ("far", 2)), (far1, far2), state, False)
    near4, *state = after(near4, *state)
    stat, out = run((("far", 3), ("near", 4)), (far3, near4), state, True)

    run = functools.partial(backward, block_perm, meta, qd, stat)
    far3, near4, dqt = run((("far", 3), ("near", 4)), (far3, near4), None, None)
    moving = send(near4, HOMEWARD)
    far3 = send(far3, CORE)
    near3, far2, dqt = run((("near", 3), ("far", 2)), (near3, far2), dqt, None)
    near2, far1, dqt = run((("near", 2), ("far", 1)), (near2, far1), dqt, None)
    moving, far2, dqt = after(moving, far2, dqt)
    moving = send(add(near3, far3, moving), HOMEWARD)
    far2 = send(far2, CORE)
    near1, own, back = run((("near", 1), ("near", 0)), (near1, own), dqt, out)
    moving, far1, own, back = after(moving, far1, own, back)
    moving = send(add(near2, far2, moving), HOMEWARD)
    far1 = send(far1, CORE)
    own_twin = send(own[2:], TWIN)
    back = lax.all_to_all(back, "head", 0, 0, tiled=True)
    moving = add(near1, far1, moving)
    attended, query_grad = relayout(join_heads, [back], [(rows, GROUP * HEAD)] * 2)
    own_twin, attended, query_grad = after(own_twin, attended, query_grad)
    pair = total32(own[:2], own_twin, *(send(moving[2 * n : 2 * n + 2], LAST_HOME[n]) for n in range(2)))
    total = add(pair[0], send(pair[1].astype(BF16), CORE))
    return attended, query_grad, total[0], total[1]


def solution(mesh):
    spec = P(("inner", "outer"), "head")
    return jax.shard_map(
        on_device,
        mesh=mesh,
        in_specs=(spec, spec, spec, spec, P(), P()),
        out_specs=(spec, spec, spec, spec),
        check_vma=False,
    )
```
